128 devices in a mesh: row: 4 (over y_lo, core), feat: 32 (over y_hi, z, x).
Axes of the slice: x: 4, y: 4 (y_hi: 2, y_lo: 2; y = y_hi * 2 + y_lo), z: 4, core: 2. Of those that a mesh axis runs over, the one named last changes fastest.
Arguments:
- activations: float32 [4, 4096, 4096], P(None, ('row', 'feat')), may hold values from -6 to 6
- out_grads: float32 [4, 4096, 4096], P(None, ('row', 'feat')), may hold values from -6 to 6
- proj_in: float32 [4096, 128], replicated, may hold values from -0.09375 to 0.09375
- proj_out: float32 [4096, 128], replicated, may hold values from -0.09375 to 0.09375
- inv_in: float32 [4, 128, 128], replicated, may hold values from -0.3 to 2, as said below
- inv_out: float32 [4, 128, 128], replicated, may hold values from -0.3 to 2, as said below
- stored: float32 [8192, 4, 16384], P('row', None, 'feat'), may hold values from -0.00390625 to 0.00390625
- query_order: int32 [128], replicated, may hold values from 0 to 127, each once
Outputs:
- scores: float32 [128, 8192], P('feat', 'row')
The draws below stay inside these ranges and needn't reach their ends.
Inputs may be any that keep to these rules, and one draw needn't show every extreme that they name: `query_order`: each query appears exactly once. `inv_in`: square matrices. `inv_out`: square matrices.
All inputs are finite; a program needn't handle non-finite values.
Results may differ from the reference program's by a relative error of at most 0.0001.
Values sent between devices are 32-bit elements; how exact they have to be, the bound alone decides.
No kernel may reach another device: no remote copies, remote signals or barrier semaphores. Data moves between devices by JAX's collectives and lax.ppermute only.
A program may use at most 128 MiB of HBM per device.

```python
import jax
import jax.numpy as jnp
from jax import lax

D_IN = 4096
D_OUT = 4096
RANK = 128
LAYERS = 4
TOK = 32
NQ = 128
STORE = 8192
FEATS = 16384


def factor_draw(key, salt):
    folded = jax.random.fold_in(key, salt)
    first_key, second_key = jax.random.split(folded)
    off_diag = jnp.clip(0.06 * jax.random.normal(first_key, (LAYERS, RANK, RANK), jnp.float32), -0.3, 0.3)
    diag_vals = jax.random.uniform(second_key, (LAYERS, RANK), jnp.float32, 0.5, 2.0)
    identity = jnp.eye(RANK, dtype=jnp.float32)
    return off_diag * (1.0 - identity) + identity * diag_vals[:, :, None]


def draw_inv_in(key, part):
    return factor_draw(key, 17)


def draw_inv_out(key, part):
    return factor_draw(key, 29)


def block_levels(own_key, shape, cuts, low, top_value):
    level, own = 1.0, jax.random.fold_in(own_key, 6)
    for position, shards_of in cuts:
        draws = jnp.exp(jax.random.uniform(jax.random.fold_in(own, position), (shards_of,), jnp.float32, low / len(cuts), top_value / len(cuts)))
        level = level * jnp.repeat(draws, shape[position] // shards_of).reshape([-1 if axis == position else 1 for axis in range(len(shape))])
    return level


def bell_draw(key, extent, width, reach, shards=(), kind=jnp.bfloat16):
    drawn = jax.random.normal(key, extent, jnp.float32) * width
    if len(shards) > 0:
        drawn = block_levels(key, extent, shards, -0.22, 0.18) * drawn
    return jnp.clip(drawn, min=-reach, max=reach).astype(kind)


def setup_inputs(seed: int = 0) -> dict:
    seeds = jax.random.split(jax.random.key(seed), 9)
    return {
        "activations": bell_draw(seeds[0], (LAYERS, NQ * TOK, D_IN), 1.0, 6.0, ((1, 128),), jnp.float32),
        "out_grads": bell_draw(seeds[1], (LAYERS, NQ * TOK, D_OUT), 1.0, 6.0, ((1, 128),), jnp.float32),
        "proj_in": bell_draw(seeds[2], (D_IN, RANK), D_IN ** -0.5, 0.09375, (), jnp.float32),
        "proj_out": bell_draw(seeds[3], (D_OUT, RANK), D_OUT ** -0.5, 0.09375, (), jnp.float32),
        "inv_in": draw_inv_in(jax.random.fold_in(seeds[8], 71), 0),
        "inv_out": draw_inv_out(jax.random.fold_in(seeds[8], 71), 0),
        "stored": bell_draw(seeds[6], (STORE, LAYERS, FEATS), (32 * LAYERS * FEATS) ** -0.5, 0.00390625, ((0, 4), (2, 32)), jnp.float32),
        "query_order": jax.random.permutation(seeds[7], NQ).astype(jnp.int32),
    }


def reference(activations, out_grads, proj_in, proj_out, inv_in, inv_out, stored, query_order):
    highest = lax.Precision.HIGHEST
    acts_low = jnp.einsum("ltd,dr->ltr", activations, proj_in, precision=highest)
    grads_low = jnp.einsum("ltd,dr->ltr", out_grads, proj_out, precision=highest)
    acts_four = acts_low.reshape(LAYERS, NQ, TOK, RANK)
    grads_four = grads_low.reshape(LAYERS, NQ, TOK, RANK)
    gradient = jnp.einsum("lqti,lqtj->lqij", grads_four, acts_four, precision=highest)
    left_side = jnp.einsum("lik,lqkj->lqij", inv_out, gradient, precision=highest)
    precond = jnp.einsum("lqik,lkj->qlij", left_side, inv_in, precision=highest)
    flat_grads = precond.reshape(NQ, LAYERS, FEATS)
    ordered = jnp.take(flat_grads, query_order, axis=0)
    return jnp.einsum("qlf,slf->qs", ordered, stored, precision=highest)
```

```python
import functools

import jax
import jax.numpy as jnp
from jax import lax
from jax.experimental import pallas as pl
from jax.experimental.pallas import tpu as pltpu
from jax.sharding import PartitionSpec as P

TOK = 32
F32, BF16 = jnp.float32, jnp.bfloat16
NN = (((1,), (0,)), ((), ()))
NT = (((1,), (1,)), ((), ()))
TN = (((0,), (0,)), ((), ()))
MIB = 1024 * 1024
WHOLE = pl.BlockSpec(memory_space=pltpu.VMEM)


def limit(mib):
    return pltpu.CompilerParams(vmem_limit_bytes=mib * MIB)


def near(x):
    return pltpu.with_memory_space_constraint(x, pltpu.VMEM)


def far(x):
    return pltpu.with_memory_space_constraint(x, pltpu.HBM)


def dot(a, b, dims=NN):
    return lax.dot_general(a, b, dims, preferred_element_type=F32)


def exact_dot(a, b, dims=NN):
    return lax.dot_general(a, b, dims, precision=lax.Precision.HIGHEST, preferred_element_type=F32)


def pieces(x):
    high = x.astype(BF16)
    return high, (x - high.astype(F32)).astype(BF16)


def wide_product(x, w):
    rows, cols = x.shape[0], w.shape[1]
    both = dot(jnp.concatenate(pieces(x), axis=0), jnp.concatenate(pieces(w), axis=1))
    return (both[rows:, cols:] + both[rows:, :cols]) + both[:rows, cols:] + both[:rows, :cols]


def precond_kernel(acts_ref, grads_ref, pin_ref, pout_ref, iin_ref, iout_ref, out_ref, acts_sum, grads_sum):
    step = pl.program_id(0)
    layers, tok, width = acts_ref.shape
    rank = pin_ref.shape[1]
    acts = wide_product(acts_ref[...].reshape(layers * tok, width), pin_ref[...])
    grads = wide_product(grads_ref[...].reshape(layers * tok, width), pout_ref[...])

    @pl.when(step == 0)
    def _():
        acts_sum[...] = acts
        grads_sum[...] = grads

    @pl.when(step > 0)
    def _():
        acts_sum[...] += acts
        grads_sum[...] += grads

    @pl.when(step == pl.num_programs(0) - 1)
    def _():
        rows, slices, per, _ = out_ref.shape
        per = per // layers
        for l in range(layers):
            mine = slice(l * tok, (l + 1) * tok)
            right = exact_dot(acts_sum[mine, :], iin_ref[l])
            left = exact_dot(grads_sum[mine, :], iout_ref[l], NT)
            cond = exact_dot(left, right, TN).reshape(slices, per, rank)
            for r in range(rows):
                out_ref[r, :, l * per : (l + 1) * per, :] = cond


def preconditioned(activations, out_grads, proj_in, proj_out, inv_in, inv_out, rows, slices, block=1024):
    layers, tok, width = activations.shape
    rank = proj_in.shape[1]
    per = rank // slices
    tokens = pl.BlockSpec((layers, tok, block), lambda k: (0, 0, k))
    side = pl.BlockSpec((block, rank), lambda k: (k, 0))
    return pl.pallas_call(
        precond_kernel,
        grid=(width // block,),
        in_specs=[tokens, tokens, side, side, WHOLE, WHOLE],
        out_specs=WHOLE,
        out_shape=pltpu.VMEM((rows, slices, layers * per, rank), F32),
        scratch_shapes=[pltpu.VMEM((layers * tok, rank), F32)] * 2,
        compiler_params=limit(8),
        name="precond",
    )(far(activations), far(out_grads), far(proj_in), far(proj_out), inv_in, inv_out)


def split_kernel(stored_ref, high_ref, low_ref):
    rows, layers, width = stored_ref.shape
    for l in range(layers):
        cols = slice(l * width, (l + 1) * width)
        high_ref[:, cols], low_ref[:, cols] = pieces(stored_ref[:, l, :])


def split_stored(stored, block=256):
    store, layers, width = stored.shape
    half = pl.BlockSpec((block, layers * width), lambda s: (s, 0))
    return pl.pallas_call(
        split_kernel,
        grid=(store // block,),
        in_specs=[pl.BlockSpec((block, layers, width), lambda s: (s, 0, 0))],
        out_specs=[half, half],
        out_shape=[pltpu.HBM((store, layers * width), BF16)] * 2,
        compiler_params=limit(16),
        cost_estimate=pl.CostEstimate(flops=stored.size * 8, bytes_accessed=stored.size * 8, transcendentals=0),
        name="split_stored",
    )(far(stored))


def scores_kernel(recv_ref, order_ref, high_ref, low_ref, out_ref, picked):
    queries, per, rank = recv_ref.shape
    slices, sub, half = out_ref.shape
    group = queries // slices
    tile = high_ref.shape[0]
    step = pl.program_id(0)

    @pl.when(step == 0)
    def _():
        ids = lax.broadcasted_iota(jnp.int32, (queries, queries), 0)
        chosen = (ids == order_ref[...]).astype(F32).astype(BF16)
        for t in range(per):
            cols = slice(t * rank, (t + 1) * rank)
            both = dot(chosen, jnp.concatenate(pieces(recv_ref[:, t, :]), axis=1), TN)
            picked[:queries, cols] = both[:, :rank].astype(BF16)
            picked[queries:, cols] = both[:, rank:].astype(BF16)

    wide = dot(picked[...], high_ref[...], NT)
    narrow = dot(picked[:queries, :], low_ref[...], NT)
    total = (wide[:queries] + (wide[queries:] + narrow)).reshape(slices, group, tile)
    each = half // tile
    cols = pl.ds(pl.multiple_of(lax.rem(step, each) * tile, tile), tile)
    for h in range(sub // group):

        @pl.when(lax.div(step, each) == h)
        def _():
            out_ref[:, h * group : (h + 1) * group, cols] = total


def partial_scores(recv, order, high, low, slices, tile=256):
    queries, per, rank = recv.shape
    store, width = high.shape
    group = queries // slices
    sub = 8
    half = store * group // sub
    piece = pl.BlockSpec((tile, width), lambda n: (n, 0))
    return pl.pallas_call(
        scores_kernel,
        grid=(store // tile,),
        in_specs=[WHOLE, WHOLE, piece, piece],
        out_specs=WHOLE,
        out_shape=pltpu.VMEM((slices, sub, half), F32),
        scratch_shapes=[pltpu.VMEM((2 * queries, width), BF16)],
        compiler_params=limit(12),
        name="scores",
    )(near(recv), order.reshape(1, queries), far(high), far(low))


def sum_kernel(parts_ref, out_ref):
    total = jnp.sum(parts_ref[...], axis=0)
    group, store = out_ref.shape
    half = parts_ref.shape[2]
    for h in range(store // half):
        out_ref[:, h * half : (h + 1) * half] = total[h * group : (h + 1) * group]


def sum_parts(parts):
    slices, sub, half = parts.shape
    group = 4
    return pl.pallas_call(
        sum_kernel,
        in_specs=[WHOLE],
        out_specs=WHOLE,
        out_shape=jax.ShapeDtypeStruct((group, sub // group * half), F32),
        name="sum_parts",
    )(near(parts))


def per_device(rows, slices, activations, out_grads, proj_in, proj_out, inv_in, inv_out, stored, query_order):
    mine = preconditioned(activations, out_grads, proj_in, proj_out, inv_in, inv_out, rows, slices)
    mine = mine.reshape((rows * slices,) + mine.shape[2:])
    recv = lax.all_to_all(mine, ("row", "feat"), 0, 0, tiled=True)
    high, low = split_stored(stored)
    parts = partial_scores(recv, query_order, high, low, slices)
    return sum_parts(lax.all_to_all(parts, "feat", 0, 0, tiled=True))


def solution(mesh):
    placed = (
        P(None, ("row", "feat"), None),
        P(None, ("row", "feat"), None),
        P(),
        P(),
        P(),
        P(),
        P("row", None, "feat"),
        P(),
    )
    return jax.shard_map(
        functools.partial(per_device, mesh.shape["row"], mesh.shape["feat"]),
        mesh=mesh,
        in_specs=placed,
        out_specs=P("feat", "row"),
        check_vma=False,
    )
```

```python
import functools

import jax
import jax.numpy as jnp
from jax import lax
from jax.experimental import pallas as pl
from jax.experimental.pallas import tpu as pltpu
from jax.sharding import PartitionSpec as P

TOK = 32
F32, BF16 = jnp.float32, jnp.bfloat16
NN = (((1,), (0,)), ((), ()))
NT = (((1,), (1,)), ((), ()))
TN = (((0,), (0,)), ((), ()))
MIB = 1024 * 1024
WHOLE = pl.BlockSpec(memory_space=pltpu.VMEM)
ANYWHERE = pl.BlockSpec(memory_space=pl.ANY)


def limit(mib):
    return pltpu.CompilerParams(vmem_limit_bytes=mib * MIB)


def near(x):
    return pltpu.with_memory_space_constraint(x, pltpu.VMEM)


def far(x):
    return pltpu.with_memory_space_constraint(x, pltpu.HBM)


def dot(a, b, dims=NN):
    return lax.dot_general(a, b, dims, preferred_element_type=F32)


def pieces(x):
    high = x.astype(BF16)
    return high, (x - high.astype(F32)).astype(BF16)


def wide_product(x, w, flip=False):
    rows, cols = x.shape[0], w.shape[0 if flip else 1]
    left, right = jnp.concatenate(pieces(x), axis=0), jnp.concatenate(pieces(w), axis=0 if flip else 1)
    both = dot(left, right, NT if flip else NN)
    return (both[rows:, cols:] + both[rows:, :cols]) + both[:rows, cols:] + both[:rows, :cols]


def precond_kernel(acts_hbm, pin_hbm, grads_hbm, pout_hbm, iin_hbm, iout_hbm, out_ref, acts, pin, grads, pout, iin, iout, sems):
    layers, tok, width = acts.shape
    rank = pin.shape[1]
    count = sems.shape[1]
    chunk = width // count

    def copies(i):
        at = pl.ds(i * chunk, chunk)
        return [
            pltpu.make_async_copy(acts_hbm.at[:, :, at], acts.at[:, :, at], sems.at[0, i]),
            pltpu.make_async_copy(pin_hbm.at[at, :], pin.at[at, :], sems.at[1, i]),
            pltpu.make_async_copy(grads_hbm.at[:, :, at], grads.at[:, :, at], sems.at[2, i]),
            pltpu.make_async_copy(pout_hbm.at[at, :], pout.at[at, :], sems.at[3, i]),
        ]

    factors = [
        pltpu.make_async_copy(iin_hbm, iin, sems.at[4, 0]),
        pltpu.make_async_copy(iout_hbm, iout, sems.at[4, 1]),
    ]
    for i in range(count):
        for copy in copies(i):
            copy.start()
    for copy in factors:
        copy.start()
    acts_low = grads_low = jnp.zeros((layers * tok, rank), F32)
    for i in range(count):
        for copy in copies(i):
            copy.wait()
        at = slice(i * chunk, (i + 1) * chunk)
        acts_low += wide_product(acts[:, :, at].reshape(layers * tok, chunk), pin[at, :])
        grads_low += wide_product(grads[:, :, at].reshape(layers * tok, chunk), pout[at, :])
    for copy in factors:
        copy.wait()
    rows, slices, per, _ = out_ref.shape
    per = per // layers
    for l in range(layers):
        mine = slice(l * tok, (l + 1) * tok)
        right = wide_product(acts_low[mine, :], iin[l])
        left = wide_product(grads_low[mine, :], iout[l], flip=True)
        (left_high, left_low), (right_high, right_low) = pieces(left), pieces(right)
        tall = jnp.concatenate([left_low, left_low, left_high, left_high], axis=0)
        other = jnp.concatenate([right_low, right_high, right_low, right_high], axis=0)
        cond = dot(tall, other, TN).reshape(slices, per, rank)
        for r in range(rows):
            out_ref[r, :, l * per : (l + 1) * per, :] = cond


def preconditioned(activations, out_grads, proj_in, proj_out, inv_in, inv_out, rows, slices, count=4):
    layers, tok, width = activations.shape
    rank = proj_in.shape[1]
    tokens = pltpu.VMEM((layers, tok, width), F32)
    side = pltpu.VMEM((width, rank), F32)
    factor = pltpu.VMEM((layers, rank, rank), F32)
    return pl.pallas_call(
        precond_kernel,
        in_specs=[ANYWHERE] * 6,
        out_specs=WHOLE,
        out_shape=pltpu.VMEM((rows, slices, layers * (rank // slices), rank), F32),
        scratch_shapes=[tokens, side, tokens, side, factor, factor, pltpu.SemaphoreType.DMA((5, count))],
        compiler_params=limit(24),
        name="precond",
    )(far(activations), far(proj_in), far(out_grads), far(proj_out), far(inv_in), far(inv_out))


def tiles_view(stored, lanes=128):
    store, layers, width = stored.shape
    runs = width // lanes
    return stored.reshape(store, layers, runs, lanes).transpose(0, 2, 1, 3).reshape(store, runs * layers, lanes)


def split_kernel(layers, tiles_hbm, high_ref, low_ref, rows, sems):
    step = pl.program_id(0)
    _, per, lanes = tiles_hbm.shape
    place = [(t % layers) * (per // layers) + t // layers for t in range(per)]
    block = rows.shape[1]

    def copies(s, slot):
        at = pl.ds(pl.multiple_of(s * block, block), block)
        return [
            pltpu.make_async_copy(tiles_hbm.at[at, t, :], rows.at[slot, :, pl.ds(place[t] * lanes, lanes)], sems.at[slot, t])
            for t in range(per)
        ]

    @pl.when(step == 0)
    def _():
        for copy in copies(0, 0):
            copy.start()

    @pl.when(step + 1 < pl.num_programs(0))
    def _():
        for copy in copies(step + 1, lax.rem(step + 1, 2)):
            copy.start()

    slot = lax.rem(step, 2)
    for copy in copies(step, slot):
        copy.wait()
    high_ref[...], low_ref[...] = pieces(rows[slot])


def split_stored(stored, block=256):
    tiles = tiles_view(stored)
    store, per, lanes = tiles.shape
    half = pl.BlockSpec((block, per * lanes), lambda s: (s, 0))
    return pl.pallas_call(
        functools.partial(split_kernel, stored.shape[1]),
        grid=(store // block,),
        in_specs=[ANYWHERE],
        out_specs=[half, half],
        out_shape=[pltpu.HBM((store, per * lanes), BF16)] * 2,
        scratch_shapes=[pltpu.VMEM((2, block, per * lanes), F32), pltpu.SemaphoreType.DMA((2, per))],
        compiler_params=limit(24),
        cost_estimate=pl.CostEstimate(flops=stored.size * 8, bytes_accessed=stored.size * 8, transcendentals=0),
        name="split_stored",
    )(far(tiles))


def scores_kernel(recv_ref, order_ref, high_hbm, low_hbm, out_ref, high, low, rows, picked, row_sems, sems):
    queries, per, rank = recv_ref.shape
    slices, sub, half = out_ref.shape
    group = queries // slices
    store = high.shape[0]
    count = sems.shape[1]
    chunk = store // count
    tile = 256

    def copies(i):
        at = pl.ds(i * chunk, chunk)
        return [
            pltpu.make_async_copy(high_hbm.at[at, :], high.at[at, :], sems.at[0, i]),
            pltpu.make_async_copy(low_hbm.at[at, :], low.at[at, :], sems.at[1, i]),
        ]

    lined = [
        pltpu.make_async_copy(recv_ref.at[:, t, :], rows.at[:, pl.ds(t * rank, rank)], row_sems.at[t])
        for t in range(per)
    ]
    for copy in lined:
        copy.start()
    for i in range(count):
        for copy in copies(i):
            copy.start()
    ids = lax.broadcasted_iota(jnp.int32, (queries, queries), 0)
    chosen = (ids == order_ref[...]).astype(F32).astype(BF16)
    for copy in lined:
        copy.wait()
    rows_high, rows_low = pieces(rows[...])
    picked[:queries, :] = dot(chosen, rows_high, TN).astype(BF16)
    picked[queries:, :] = dot(chosen, rows_low, TN).astype(BF16)
    for n in range(store // tile):
        if n * tile % chunk == 0:
            for copy in copies(n * tile // chunk):
                copy.wait()
        at = slice(n * tile, (n + 1) * tile)
        wide = dot(high[at, :], picked[...], NT)
        narrow = dot(low[at, :], picked[:queries, :], NT)
        total = (wide[:, :queries] + (wide[:, queries:] + narrow)).T
        h, c = divmod(n * tile, half)
        out_ref[:, h * group : (h + 1) * group, c : c + tile] = total.reshape(slices, group, tile)


def partial_scores(recv, order, high, low, slices, count=4):
    queries, per, rank = recv.shape
    store, width = high.shape
    sub = 8
    half = store * (queries // slices) // sub
    return pl.pallas_call(
        scores_kernel,
        in_specs=[WHOLE, WHOLE, ANYWHERE, ANYWHERE],
        out_specs=WHOLE,
        out_shape=pltpu.VMEM((slices, sub, half), F32),
        scratch_shapes=[
            pltpu.VMEM((store, width), BF16),
            pltpu.VMEM((store, width), BF16),
            pltpu.VMEM((queries, width), F32),
            pltpu.VMEM((2 * queries, width), BF16),
            pltpu.SemaphoreType.DMA((per,)),
            pltpu.SemaphoreType.DMA((2, count)),
        ],
        compiler_params=limit(32),
        name="scores",
    )(near(recv), order.reshape(1, queries), far(high), far(low))


def sum_kernel(parts_ref, out_ref):
    total = jnp.sum(parts_ref[...], axis=0)
    group, store = out_ref.shape
    half = parts_ref.shape[2]
    for h in range(store // half):
        out_ref[:, h * half : (h + 1) * half] = total[h * group : (h + 1) * group]


def sum_parts(parts):
    slices, sub, half = parts.shape
    group = 4
    return pl.pallas_call(
        sum_kernel,
        in_specs=[WHOLE],
        out_specs=WHOLE,
        out_shape=jax.ShapeDtypeStruct((group, sub // group * half), F32),
        name="sum_parts",
    )(near(parts))


def per_device(rows, slices, activations, out_grads, proj_in, proj_out, inv_in, inv_out, stored, query_order):
    mine = preconditioned(activations, out_grads, proj_in, proj_out, inv_in, inv_out, rows, slices)
    mine = mine.reshape((rows * slices,) + mine.shape[2:])
    recv = lax.all_to_all(mine, ("row", "feat"), 0, 0, tiled=True)
    high, low = split_stored(stored)
    parts = partial_scores(recv, query_order, high, low, slices)
    return sum_parts(lax.all_to_all(parts, "feat", 0, 0, tiled=True))


def solution(mesh):
    placed = (
        P(None, ("row", "feat"), None),
        P(None, ("row", "feat"), None),
        P(),
        P(),
        P(),
        P(),
        P("row", None, "feat"),
        P(),
    )
    return jax.shard_map(
        functools.partial(per_device, mesh.shape["row"], mesh.shape["feat"]),
        mesh=mesh,
        in_specs=placed,
        out_specs=P("feat", "row"),
        check_vma=False,
    )
```

```python
import functools

import jax
import jax.numpy as jnp
from jax import lax
from jax.experimental import pallas as pl
from jax.experimental.pallas import tpu as pltpu
from jax.sharding import PartitionSpec as P

TOK = 32
F32, BF16 = jnp.float32, jnp.bfloat16
NN = (((1,), (0,)), ((), ()))
NT = (((1,), (1,)), ((), ()))
TN = (((0,), (0,)), ((), ()))
MIB = 1024 * 1024
WHOLE = pl.BlockSpec(memory_space=pltpu.VMEM)
ANYWHERE = pl.BlockSpec(memory_space=pl.ANY)


def limit(mib):
    return pltpu.CompilerParams(vmem_limit_bytes=mib * MIB)


def near(x):
    return pltpu.with_memory_space_constraint(x, pltpu.VMEM)


def far(x):
    return pltpu.with_memory_space_constraint(x, pltpu.HBM)


def dot(a, b, dims=NN):
    return lax.dot_general(a, b, dims, preferred_element_type=F32)


def pieces(x):
    high = x.astype(BF16)
    return high, (x - high.astype(F32)).astype(BF16)


def wide_product(x, w, flip=False):
    rows, cols = x.shape[0], w.shape[0 if flip else 1]
    left, right = jnp.concatenate(pieces(x), axis=0), jnp.concatenate(pieces(w), axis=0 if flip else 1)
    both = dot(left, right, NT if flip else NN)
    return (both[rows:, cols:] + both[rows:, :cols]) + both[:rows, cols:] + both[:rows, :cols]


def project_kernel(acts_hbm, pin_hbm, grads_hbm, pout_hbm, acts_low_ref, grads_low_ref, acts, pin, grads, pout, sems):
    layers, tok, width = acts.shape
    rank = pin.shape[1]
    count = sems.shape[1]
    chunk = width // count

    def copies(i):
        at = pl.ds(i * chunk, chunk)
        return [
            pltpu.make_async_copy(acts_hbm.at[:, :, at], acts.at[:, :, at], sems.at[0, i]),
            pltpu.make_async_copy(pin_hbm.at[at, :], pin.at[at, :], sems.at[1, i]),
            pltpu.make_async_copy(grads_hbm.at[:, :, at], grads.at[:, :, at], sems.at[2, i]),
            pltpu.make_async_copy(pout_hbm.at[at, :], pout.at[at, :], sems.at[3, i]),
        ]

    for i in range(count):
        for copy in copies(i):
            copy.start()
    acts_low = grads_low = jnp.zeros((layers * tok, rank), F32)
    for i in range(count):
        for copy in copies(i):
            copy.wait()
        at = slice(i * chunk, (i + 1) * chunk)
        acts_low += wide_product(acts[:, :, at].reshape(layers * tok, chunk), pin[at, :])
        grads_low += wide_product(grads[:, :, at].reshape(layers * tok, chunk), pout[at, :])
    acts_low_ref[...] = acts_low
    grads_low_ref[...] = grads_low


def projected(activations, out_grads, proj_in, proj_out, count=4):
    layers, tok, width = activations.shape
    rank = proj_in.shape[1]
    tokens = pltpu.VMEM((layers, tok, width), F32)
    side = pltpu.VMEM((width, rank), F32)
    return pl.pallas_call(
        project_kernel,
        in_specs=[ANYWHERE] * 4,
        out_specs=[WHOLE] * 2,
        out_shape=[pltpu.VMEM((layers * tok, rank), F32)] * 2,
        scratch_shapes=[tokens, side, tokens, side, pltpu.SemaphoreType.DMA((4, count))],
        compiler_params=limit(12),
        name="projected",
    )(far(activations), far(proj_in), far(out_grads), far(proj_out))


def precond_kernel(acts_low, grads_low, iin, iout, out_ref):
    rows, slices, per, rank = out_ref.shape
    layers = iin.shape[0]
    tok = acts_low.shape[0] // layers
    per = per // layers
    for l in range(layers):
        mine = slice(l * tok, (l + 1) * tok)
        right = wide_product(acts_low[mine, :], iin[l])
        left = wide_product(grads_low[mine, :], iout[l], flip=True)
        (left_high, left_low), (right_high, right_low) = pieces(left), pieces(right)
        tall = jnp.concatenate([left_low, left_low, left_high, left_high], axis=0)
        other = jnp.concatenate([right_low, right_high, right_low, right_high], axis=0)
        cond = dot(tall, other, TN).reshape(slices, per, rank)
        for r in range(rows):
            out_ref[r, :, l * per : (l + 1) * per, :] = cond


def preconditioned(acts_low, grads_low, inv_in, inv_out, rows, slices):
    layers, rank, _ = inv_in.shape
    return pl.pallas_call(
        precond_kernel,
        in_specs=[WHOLE] * 4,
        out_specs=WHOLE,
        out_shape=pltpu.VMEM((rows, slices, layers * (rank // slices), rank), F32),
        compiler_params=limit(4),
        cost_estimate=pl.CostEstimate(flops=1 << 33, bytes_accessed=1 << 20, transcendentals=0),
        name="precond",
    )(near(acts_low), near(grads_low), near(inv_in), near(inv_out))


def tiles_view(stored, lanes=128):
    store, layers, width = stored.shape
    runs = width // lanes
    return stored.reshape(store, layers, runs, lanes).transpose(0, 2, 1, 3).reshape(store, runs * layers, lanes)


def scores_kernel(layers, recv_ref, order_ref, tiles_ref, out_ref, rows, picked, sems):
    queries, per, rank = recv_ref.shape
    slices, sub, half = out_ref.shape
    group = queries // slices
    store = tiles_ref.shape[0]
    runs = per // layers
    tile = 256
    lined = []
    for t in range(per):
        place = (t % runs) * layers + t // runs
        lined.append(pltpu.make_async_copy(recv_ref.at[:, t, :], rows.at[:, pl.ds(place * rank, rank)], sems.at[t]))
    for copy in lined:
        copy.start()
    ids = lax.broadcasted_iota(jnp.int32, (queries, queries), 0)
    chosen = (ids == order_ref[...]).astype(F32).astype(BF16)
    for copy in lined:
        copy.wait()
    rows_high, rows_low = pieces(rows[...])
    picked[:queries, :] = dot(chosen, rows_high, TN).astype(BF16)
    picked[queries:, :] = dot(chosen, rows_low, TN).astype(BF16)
    for n in range(store // tile):
        high, low = pieces(tiles_ref[n * tile : (n + 1) * tile].reshape(tile, per * rank))
        wide = dot(high, picked[...], NT)
        narrow = dot(low, picked[:queries, :], NT)
        total = (wide[:, :queries] + (wide[:, queries:] + narrow)).T
        h, c = divmod(n * tile, half)
        out_ref[:, h * group : (h + 1) * group, c : c + tile] = total.reshape(slices, group, tile)


def partial_scores(recv, order, stored, slices):
    queries, per, rank = recv.shape
    store, layers, _ = stored.shape
    sub = 8
    half = store * (queries // slices) // sub
    return pl.pallas_call(
        functools.partial(scores_kernel, layers),
        in_specs=[WHOLE] * 3,
        out_specs=WHOLE,
        out_shape=pltpu.VMEM((slices, sub, half), F32),
        scratch_shapes=[
            pltpu.VMEM((queries, per * rank), F32),
            pltpu.VMEM((2 * queries, per * rank), BF16),
            pltpu.SemaphoreType.DMA((per,)),
        ],
        compiler_params=limit(4),
        name="scores",
    )(near(recv), order.reshape(1, queries), near(tiles_view(stored)))


def sum_kernel(parts_ref, out_ref):
    total = jnp.sum(parts_ref[...], axis=0)
    group, store = out_ref.shape
    half = parts_ref.shape[2]
    for h in range(store // half):
        out_ref[:, h * half : (h + 1) * half] = total[h * group : (h + 1) * group]


def sum_parts(parts):
    slices, sub, half = parts.shape
    group = 4
    return pl.pallas_call(
        sum_kernel,
        in_specs=[WHOLE],
        out_specs=WHOLE,
        out_shape=jax.ShapeDtypeStruct((group, sub // group * half), F32),
        name="sum_parts",
    )(near(parts))


def per_device(rows, slices, activations, out_grads, proj_in, proj_out, inv_in, inv_out, stored, query_order):
    acts_low, grads_low = projected(activations, out_grads, proj_in, proj_out)
    mine = preconditioned(acts_low, grads_low, inv_in, inv_out, rows, slices)
    mine = mine.reshape((rows * slices,) + mine.shape[2:])
    recv = lax.all_to_all(mine, ("row", "feat"), 0, 0, tiled=True)
    parts = partial_scores(recv, query_order, stored, slices)
    return sum_parts(lax.all_to_all(parts, "feat", 0, 0, tiled=True))


def solution(mesh):
    placed = (
        P(None, ("row", "feat"), None),
        P(None, ("row", "feat"), None),
        P(),
        P(),
        P(),
        P(),
        P("row", None, "feat"),
        P(),
    )
    return jax.shard_map(
        functools.partial(per_device, mesh.shape["row"], mesh.shape["feat"]),
        mesh=mesh,
        in_specs=placed,
        out_specs=P("feat", "row"),
        check_vma=False,
    )
```

```python
import functools

import jax
import jax.numpy as jnp
from jax import lax
from jax.experimental import pallas as pl
from jax.experimental.pallas import tpu as pltpu
from jax.sharding import PartitionSpec as P

ROWS, CORES = 4, 2
F32, BF16 = jnp.float32, jnp.bfloat16
NN = (((1,), (0,)), ((), ()))
NT = (((1,), (1,)), ((), ()))
TN = (((0,), (0,)), ((), ()))
MIB = 1024 * 1024
WHOLE = pl.BlockSpec(memory_space=pltpu.VMEM)
ANYWHERE = pl.BlockSpec(memory_space=pl.ANY)


def limit(mib):
    return pltpu.CompilerParams(vmem_limit_bytes=mib * MIB)


def near(x):
    return pltpu.with_memory_space_constraint(x, pltpu.VMEM)


def far(x):
    return pltpu.with_memory_space_constraint(x, pltpu.HBM)


def dot(a, b, dims=NN):
    return lax.dot_general(a, b, dims, preferred_element_type=F32)


def pieces(x):
    high = x.astype(BF16)
    return high, (x - high.astype(F32)).astype(BF16)


def wide_product(x, w, flip=False):
    rows, cols = x.shape[0], w.shape[0 if flip else 1]
    left, right = jnp.concatenate(pieces(x), axis=0), jnp.concatenate(pieces(w), axis=0 if flip else 1)
    both = dot(left, right, NT if flip else NN)
    return (both[rows:, cols:] + both[rows:, :cols]) + both[:rows, cols:] + both[:rows, :cols]


def project_kernel(acts_hbm, pin_hbm, grads_hbm, pout_hbm, acts_low_ref, grads_low_ref, acts, pin, grads, pout, sems):
    layers, tok, width = acts.shape
    rank = pin.shape[1]
    count = sems.shape[1]
    chunk = width // count

    def copies(i):
        at = pl.ds(i * chunk, chunk)
        return [
            pltpu.make_async_copy(acts_hbm.at[:, :, at], acts.at[:, :, at], sems.at[0, i]),
            pltpu.make_async_copy(pin_hbm.at[at, :], pin.at[at, :], sems.at[1, i]),
            pltpu.make_async_copy(grads_hbm.at[:, :, at], grads.at[:, :, at], sems.at[2, i]),
            pltpu.make_async_copy(pout_hbm.at[at, :], pout.at[at, :], sems.at[3, i]),
        ]

    for i in range(count):
        for copy in copies(i):
            copy.start()
    acts_low = grads_low = jnp.zeros((layers * tok, rank), F32)
    for i in range(count):
        for copy in copies(i):
            copy.wait()
        at = slice(i * chunk, (i + 1) * chunk)
        acts_low += wide_product(acts[:, :, at].reshape(layers * tok, chunk), pin[at, :])
        grads_low += wide_product(grads[:, :, at].reshape(layers * tok, chunk), pout[at, :])
    acts_low_ref[...] = acts_low
    grads_low_ref[...] = grads_low


def projected(activations, out_grads, proj_in, proj_out, count=4):
    layers, tok, width = activations.shape
    rank = proj_in.shape[1]
    tokens = pltpu.VMEM((layers, tok, width), F32)
    side = pltpu.VMEM((width, rank), F32)
    return pl.pallas_call(
        project_kernel,
        in_specs=[ANYWHERE] * 4,
        out_specs=[WHOLE] * 2,
        out_shape=[pltpu.VMEM((layers * tok, rank), F32)] * 2,
        scratch_shapes=[tokens, side, tokens, side, pltpu.SemaphoreType.DMA((4, count))],
        compiler_params=limit(12),
        name="projected",
    )(far(activations), far(proj_in), far(out_grads), far(proj_out))


def precond_kernel(acts_low, grads_low, iin, iout, out_ref):
    rows, slices, per, rank = out_ref.shape
    layers = iin.shape[0]
    tok = acts_low.shape[0] // layers
    per = per // layers
    for l in range(layers):
        mine = slice(l * tok, (l + 1) * tok)
        right = wide_product(acts_low[mine, :], iin[l])
        left = wide_product(grads_low[mine, :], iout[l], flip=True)
        (left_high, left_low), (right_high, right_low) = pieces(left), pieces(right)
        tall = jnp.concatenate([left_low, left_low, left_high, left_high], axis=0)
        other = jnp.concatenate([right_low, right_high, right_low, right_high], axis=0)
        cond = dot(tall, other, TN).reshape(slices, per, rank)
        for r in range(rows):
            out_ref[r, :, l * per : (l + 1) * per, :] = cond


def preconditioned(acts_low, grads_low, inv_in, inv_out, rows, slices):
    layers, rank, _ = inv_in.shape
    return pl.pallas_call(
        precond_kernel,
        in_specs=[WHOLE] * 4,
        out_specs=WHOLE,
        out_shape=pltpu.VMEM((rows, slices, layers * (rank // slices), rank), F32),
        compiler_params=limit(4),
        cost_estimate=pl.CostEstimate(flops=1 << 33, bytes_accessed=1 << 20, transcendentals=0),
        name="precond",
    )(near(acts_low), near(grads_low), near(inv_in), near(inv_out))


def tiles_view(stored, lanes=128):
    store, layers, width = stored.shape
    runs = width // lanes
    return stored.reshape(store, layers, runs, lanes).transpose(0, 2, 1, 3).reshape(store, runs * layers, lanes)


def positions(order, slices, mine):
    bits = slices.bit_length() - 1
    row = lax.shift_right_logical(order, bits)
    other = jnp.where((row & (CORES - 1)) == mine, 0, 1)
    pairs = ROWS // CORES
    return (other * pairs + lax.shift_right_logical(row, CORES.bit_length() - 1)) * slices + (order & (slices - 1))


def scores_kernel(layers, recv_ref, swapped_ref, order_ref, tiles_ref, out_ref, rows, picked, sems):
    held, per, rank = recv_ref.shape
    queries = CORES * held
    slices, sub, half = out_ref.shape
    group = queries // slices
    store = tiles_ref.shape[0]
    runs = per // layers
    tile = 256
    lined = []
    for t in range(per):
        place = (t % runs) * layers + t // runs
        for c, part in enumerate((recv_ref, swapped_ref)):
            to = rows.at[pl.ds(c * held, held), pl.ds(place * rank, rank)]
            lined.append(pltpu.make_async_copy(part.at[:, t, :], to, sems.at[c, t]))
    for copy in lined:
        copy.start()
    ids = lax.broadcasted_iota(jnp.int32, (queries, queries), 0)
    at = positions(order_ref[...], slices, lax.rem(lax.axis_index("row"), CORES))
    chosen = (ids == at).astype(F32).astype(BF16)
    for copy in lined:
        copy.wait()
    rows_high, rows_low = pieces(rows[...])
    picked[:queries, :] = dot(chosen, rows_high, TN).astype(BF16)
    picked[queries:, :] = dot(chosen, rows_low, TN).astype(BF16)
    for n in range(store // tile):
        high, low = pieces(tiles_ref[n * tile : (n + 1) * tile].reshape(tile, per * rank))
        wide = dot(high, picked[...], NT)
        narrow = dot(low, picked[:queries, :], NT)
        total = (wide[:, :queries] + (wide[:, queries:] + narrow)).T
        h, c = divmod(n * tile, half)
        out_ref[:, h * group : (h + 1) * group, c : c + tile] = total.reshape(slices, group, tile)


def partial_scores(recv, swapped, order, stored, slices):
    held, per, rank = recv.shape
    queries = CORES * held
    store, layers, _ = stored.shape
    sub = 8
    half = store * (queries // slices) // sub
    return pl.pallas_call(
        functools.partial(scores_kernel, layers),
        in_specs=[WHOLE] * 4,
        out_specs=WHOLE,
        out_shape=pltpu.VMEM((slices, sub, half), F32),
        scratch_shapes=[
            pltpu.VMEM((queries, per * rank), F32),
            pltpu.VMEM((2 * queries, per * rank), BF16),
            pltpu.SemaphoreType.DMA((CORES, per)),
        ],
        compiler_params=limit(4),
        name="scores",
    )(near(recv), near(swapped), order.reshape(1, queries), near(tiles_view(stored)))


def sum_kernel(parts_ref, out_ref):
    total = jnp.sum(parts_ref[...], axis=0)
    group, store = out_ref.shape
    half = parts_ref.shape[2]
    for h in range(store // half):
        out_ref[:, h * half : (h + 1) * half] = total[h * group : (h + 1) * group]


def sum_parts(parts):
    slices, sub, half = parts.shape
    group = 4
    return pl.pallas_call(
        sum_kernel,
        in_specs=[WHOLE],
        out_specs=WHOLE,
        out_shape=jax.ShapeDtypeStruct((group, sub // group * half), F32),
        name="sum_parts",
    )(near(parts))


def per_device(slices, activations, out_grads, proj_in, proj_out, inv_in, inv_out, stored, query_order):
    acts_low, grads_low = projected(activations, out_grads, proj_in, proj_out)
    mine = preconditioned(acts_low, grads_low, inv_in, inv_out, ROWS // CORES, slices)
    mine = mine.reshape((-1,) + mine.shape[2:])
    alike = [[r * slices + f for r in range(c, ROWS, CORES) for f in range(slices)] for c in range(CORES)]
    recv = lax.all_to_all(mine, ("row", "feat"), 0, 0, tiled=True, axis_index_groups=alike)
    swapped = lax.ppermute(recv, "row", [(r, r ^ 1) for r in range(ROWS)])
    parts = partial_scores(recv, swapped, query_order, stored, slices)
    return sum_parts(lax.all_to_all(parts, "feat", 0, 0, tiled=True))


def solution(mesh):
    placed = (
        P(None, ("row", "feat"), None),
        P(None, ("row", "feat"), None),
        P(),
        P(),
        P(),
        P(),
        P("row", None, "feat"),
        P(),
    )
    return jax.shard_map(
        functools.partial(per_device, mesh.shape["feat"]),
        mesh=mesh,
        in_specs=placed,
        out_specs=P("feat", "row"),
        check_vma=False,
    )
```

```python
import functools

import jax
import jax.numpy as jnp
from jax import lax
from jax.experimental import pallas as pl
from jax.experimental.pallas import tpu as pltpu
from jax.sharding import PartitionSpec as P

ROWS, CORES = 4, 2
F32, BF16 = jnp.float32, jnp.bfloat16
NN = (((1,), (0,)), ((), ()))
NT = (((1,), (1,)), ((), ()))
TN = (((0,), (0,)), ((), ()))
MIB = 1024 * 1024
WHOLE = pl.BlockSpec(memory_space=pltpu.VMEM)
ANYWHERE = pl.BlockSpec(memory_space=pl.ANY)


def limit(mib):
    return pltpu.CompilerParams(vmem_limit_bytes=mib * MIB)


def near(x):
    return pltpu.with_memory_space_constraint(x, pltpu.VMEM)


def far(x):
    return pltpu.with_memory_space_constraint(x, pltpu.HBM)


def dot(a, b, dims=NN):
    return lax.dot_general(a, b, dims, preferred_element_type=F32)


def pieces(x):
    high = x.astype(BF16)
    return high, (x - high.astype(F32)).astype(BF16)


def wide_product(x, w, flip=False):
    rows, cols = x.shape[0], w.shape[0 if flip else 1]
    left, right = jnp.concatenate(pieces(x), axis=0), jnp.concatenate(pieces(w), axis=0 if flip else 1)
    both = dot(left, right, NT if flip else NN)
    return (both[rows:, cols:] + both[rows:, :cols]) + both[:rows, cols:] + both[:rows, :cols]


def project_kernel(acts_hbm, pin_hbm, grads_hbm, pout_hbm, acts_low_ref, grads_low_ref, acts, pin, grads, pout, sems):
    layers, tok, width = acts.shape
    rank = pin.shape[1]
    count = sems.shape[1]
    chunk = width // count

    def copies(i):
        at = pl.ds(i * chunk, chunk)
        return [
            pltpu.make_async_copy(acts_hbm.at[:, :, at], acts.at[:, :, at], sems.at[0, i]),
            pltpu.make_async_copy(pin_hbm.at[at, :], pin.at[at, :], sems.at[1, i]),
            pltpu.make_async_copy(grads_hbm.at[:, :, at], grads.at[:, :, at], sems.at[2, i]),
            pltpu.make_async_copy(pout_hbm.at[at, :], pout.at[at, :], sems.at[3, i]),
        ]

    for i in range(count):
        for copy in copies(i):
            copy.start()
    acts_low = grads_low = jnp.zeros((layers * tok, rank), F32)
    for i in range(count):
        for copy in copies(i):
            copy.wait()
        at = slice(i * chunk, (i + 1) * chunk)
        acts_low += wide_product(acts[:, :, at].reshape(layers * tok, chunk), pin[at, :])
        grads_low += wide_product(grads[:, :, at].reshape(layers * tok, chunk), pout[at, :])
    acts_low_ref[...] = acts_low
    grads_low_ref[...] = grads_low


def projected(activations, out_grads, proj_in, proj_out, count=4):
    layers, tok, width = activations.shape
    rank = proj_in.shape[1]
    tokens = pltpu.VMEM((layers, tok, width), F32)
    side = pltpu.VMEM((width, rank), F32)
    return pl.pallas_call(
        project_kernel,
        in_specs=[ANYWHERE] * 4,
        out_specs=[WHOLE] * 2,
        out_shape=[pltpu.VMEM((layers * tok, rank), F32)] * 2,
        scratch_shapes=[tokens, side, tokens, side, pltpu.SemaphoreType.DMA((4, count))],
        compiler_params=limit(12),
        name="projected",
    )(far(activations), far(proj_in), far(out_grads), far(proj_out))


def precond_kernel(acts_low, grads_low, iin, iout, out_ref):
    rows, slices, per, rank = out_ref.shape
    layers = iin.shape[0]
    tok = acts_low.shape[0] // layers
    runs = per // layers
    each = []
    for l in range(layers):
        mine = slice(l * tok, (l + 1) * tok)
        right = wide_product(acts_low[mine, :], iin[l])
        left = wide_product(grads_low[mine, :], iout[l], flip=True)
        (left_high, left_low), (right_high, right_low) = pieces(left), pieces(right)
        tall = jnp.concatenate([left_low, left_low, left_high, left_high], axis=0)
        other = jnp.concatenate([right_low, right_high, right_low, right_high], axis=0)
        each.append(dot(tall, other, TN).reshape(slices, runs, 1, rank))
    cond = jnp.concatenate(each, axis=2).reshape(slices, per, rank)
    for r in range(rows):
        out_ref[r] = cond


def preconditioned(acts_low, grads_low, inv_in, inv_out, rows, slices):
    layers, rank, _ = inv_in.shape
    return pl.pallas_call(
        precond_kernel,
        in_specs=[WHOLE] * 4,
        out_specs=WHOLE,
        out_shape=pltpu.VMEM((rows, slices, layers * (rank // slices), rank), F32),
        compiler_params=limit(4),
        cost_estimate=pl.CostEstimate(flops=1 << 33, bytes_accessed=1 << 20, transcendentals=0),
        name="precond",
    )(near(acts_low), near(grads_low), near(inv_in), near(inv_out))


def tiles_view(stored, lanes=128):
    store, layers, width = stored.shape
    runs = width // lanes
    return stored.reshape(store, layers, runs, lanes).transpose(0, 2, 1, 3).reshape(store, runs * layers, lanes)


def positions(order, slices, mine):
    bits = slices.bit_length() - 1
    row = lax.shift_right_logical(order, bits)
    other = jnp.where((row & (CORES - 1)) == mine, 0, 1)
    pairs = ROWS // CORES
    return (other * pairs + lax.shift_right_logical(row, CORES.bit_length() - 1)) * slices + (order & (slices - 1))


def scores_kernel(recv_ref, swapped_ref, order_ref, tiles_ref, out_ref, picked):
    held, per, rank = recv_ref.shape
    queries = CORES * held
    slices, sub, half = out_ref.shape
    group = queries // slices
    store = tiles_ref.shape[0]
    tile = 256
    ids = lax.broadcasted_iota(jnp.int32, (queries, queries), 0)
    at = positions(order_ref[...], slices, lax.rem(lax.axis_index("row"), CORES))
    chosen = (ids == at).astype(F32).astype(BF16)
    rows = jnp.concatenate([ref[...].reshape(held, per * rank) for ref in (recv_ref, swapped_ref)], axis=0)
    rows_high, rows_low = pieces(rows)
    picked[:queries, :] = dot(chosen, rows_high, TN).astype(BF16)
    picked[queries:, :] = dot(chosen, rows_low, TN).astype(BF16)
    for n in range(store // tile):
        high, low = pieces(tiles_ref[n * tile : (n + 1) * tile].reshape(tile, per * rank))
        wide = dot(high, picked[...], NT)
        narrow = dot(low, picked[:queries, :], NT)
        total = (wide[:, :queries] + (wide[:, queries:] + narrow)).T
        h, c = divmod(n * tile, half)
        out_ref[:, h * group : (h + 1) * group, c : c + tile] = total.reshape(slices, group, tile)


def partial_scores(recv, swapped, order, stored, slices):
    held, per, rank = recv.shape
    queries = CORES * held
    store = stored.shape[0]
    sub = 8
    half = store * (queries // slices) // sub
    return pl.pallas_call(
        scores_kernel,
        in_specs=[WHOLE] * 4,
        out_specs=WHOLE,
        out_shape=pltpu.VMEM((slices, sub, half), F32),
        scratch_shapes=[pltpu.VMEM((2 * queries, per * rank), BF16)],
        compiler_params=limit(4),
        name="scores",
    )(near(recv), near(swapped), order.reshape(1, queries), near(tiles_view(stored)))


def sum_kernel(parts_ref, out_ref):
    total = jnp.sum(parts_ref[...], axis=0)
    group, store = out_ref.shape
    half = parts_ref.shape[2]
    for h in range(store // half):
        out_ref[:, h * half : (h + 1) * half] = total[h * group : (h + 1) * group]


def sum_parts(parts):
    slices, sub, half = parts.shape
    group = 4
    return pl.pallas_call(
        sum_kernel,
        in_specs=[WHOLE],
        out_specs=WHOLE,
        out_shape=jax.ShapeDtypeStruct((group, sub // group * half), F32),
        name="sum_parts",
    )(near(parts))


def per_device(slices, activations, out_grads, proj_in, proj_out, inv_in, inv_out, stored, query_order):
    acts_low, grads_low = projected(activations, out_grads, proj_in, proj_out)
    mine = preconditioned(acts_low, grads_low, inv_in, inv_out, ROWS // CORES, slices)
    mine = mine.reshape((-1,) + mine.shape[2:])
    alike = [[r * slices + f for r in range(c, ROWS, CORES) for f in range(slices)] for c in range(CORES)]
    recv = lax.all_to_all(mine, ("row", "feat"), 0, 0, tiled=True, axis_index_groups=alike)
    swapped = lax.ppermute(recv, "row", [(r, r ^ 1) for r in range(ROWS)])
    parts = partial_scores(recv, swapped, query_order, stored, slices)
    return sum_parts(lax.all_to_all(parts, "feat", 0, 0, tiled=True))


def solution(mesh):
    placed = (
        P(None, ("row", "feat"), None),
        P(None, ("row", "feat"), None),
        P(),
        P(),
        P(),
        P(),
        P("row", None, "feat"),
        P(),
    )
    return jax.shard_map(
        functools.partial(per_device, mesh.shape["feat"]),
        mesh=mesh,
        in_specs=placed,
        out_specs=P("feat", "row"),
        check_vma=False,
    )
```

```python
import functools

import jax
import jax.numpy as jnp
from jax import lax
from jax.experimental import pallas as pl
from jax.experimental.pallas import tpu as pltpu
from jax.sharding import PartitionSpec as P

ROWS, CORES = 4, 2
F32, BF16 = jnp.float32, jnp.bfloat16
NN = (((1,), (0,)), ((), ()))
NT = (((1,), (1,)), ((), ()))
TN = (((0,), (0,)), ((), ()))
MIB = 1024 * 1024
WHOLE = pl.BlockSpec(memory_space=pltpu.VMEM)
ANYWHERE = pl.BlockSpec(memory_space=pl.ANY)


def limit(mib):
    return pltpu.CompilerParams(vmem_limit_bytes=mib * MIB)


def near(x):
    return pltpu.with_memory_space_constraint(x, pltpu.VMEM)


def far(x):
    return pltpu.with_memory_space_constraint(x, pltpu.HBM)


def dot(a, b, dims=NN):
    return lax.dot_general(a, b, dims, preferred_element_type=F32)


def pieces(x):
    high = x.astype(BF16)
    return high, (x - high.astype(F32)).astype(BF16)


def wide_product(x, w, flip=False):
    rows, cols = x.shape[0], w.shape[0 if flip else 1]
    left, right = jnp.concatenate(pieces(x), axis=0), jnp.concatenate(pieces(w), axis=0 if flip else 1)
    both = dot(left, right, NT if flip else NN)
    return (both[rows:, cols:] + both[rows:, :cols]) + both[:rows, cols:] + both[:rows, :cols]


def project_kernel(acts_hbm, pin_hbm, grads_hbm, pout_hbm, acts_low_ref, grads_low_ref, acts, pin, grads, pout, sems):
    layers, tok, width = acts.shape
    rank = pin.shape[1]
    count = sems.shape[1]
    chunk = width // count

    def copies(i):
        at = pl.ds(i * chunk, chunk)
        return [
            pltpu.make_async_copy(acts_hbm.at[:, :, at], acts.at[:, :, at], sems.at[0, i]),
            pltpu.make_async_copy(pin_hbm.at[at, :], pin.at[at, :], sems.at[1, i]),
            pltpu.make_async_copy(grads_hbm.at[:, :, at], grads.at[:, :, at], sems.at[2, i]),
            pltpu.make_async_copy(pout_hbm.at[at, :], pout.at[at, :], sems.at[3, i]),
        ]

    for i in range(count):
        for copy in copies(i):
            copy.start()
    acts_low = grads_low = jnp.zeros((layers * tok, rank), F32)
    for i in range(count):
        for copy in copies(i):
            copy.wait()
        at = slice(i * chunk, (i + 1) * chunk)
        acts_low += wide_product(acts[:, :, at].reshape(layers * tok, chunk), pin[at, :])
        grads_low += wide_product(grads[:, :, at].reshape(layers * tok, chunk), pout[at, :])
    acts_low_ref[...] = acts_low
    grads_low_ref[...] = grads_low


def projected(activations, out_grads, proj_in, proj_out, count=4):
    layers, tok, width = activations.shape
    rank = proj_in.shape[1]
    tokens = pltpu.VMEM((layers, tok, width), F32)
    side = pltpu.VMEM((width, rank), F32)
    return pl.pallas_call(
        project_kernel,
        in_specs=[ANYWHERE] * 4,
        out_specs=[WHOLE] * 2,
        out_shape=[pltpu.VMEM((layers * tok, rank), F32)] * 2,
        scratch_shapes=[tokens, side, tokens, side, pltpu.SemaphoreType.DMA((4, count))],
        compiler_params=limit(12),
        name="projected",
    )(far(activations), far(proj_in), far(out_grads), far(proj_out))


def precond_kernel(acts_low, grads_low, iin, iout, out_ref):
    rows, slices, part, rank = out_ref.shape
    per = CORES * part
    layers = iin.shape[0]
    tok = acts_low.shape[0] // layers
    runs = per // layers
    each = []
    for l in range(layers):
        mine = slice(l * tok, (l + 1) * tok)
        right = wide_product(acts_low[mine, :], iin[l])
        left = wide_product(grads_low[mine, :], iout[l], flip=True)
        (left_high, left_low), (right_high, right_low) = pieces(left), pieces(right)
        tall = jnp.concatenate([left_low, left_low, left_high, left_high], axis=0)
        other = jnp.concatenate([right_low, right_high, right_low, right_high], axis=0)
        each.append(dot(tall, other, TN).reshape(slices, runs, 1, rank))
    cond = jnp.concatenate(each, axis=2).reshape(slices, per, rank)
    for r in range(rows):
        c = r % CORES
        out_ref[r] = cond[:, c * part : (c + 1) * part, :]


def preconditioned(acts_low, grads_low, inv_in, inv_out, rows, slices):
    layers, rank, _ = inv_in.shape
    return pl.pallas_call(
        precond_kernel,
        in_specs=[WHOLE] * 4,
        out_specs=WHOLE,
        out_shape=pltpu.VMEM((rows, slices, layers * (rank // slices) // CORES, rank), F32),
        compiler_params=limit(4),
        cost_estimate=pl.CostEstimate(flops=1 << 33, bytes_accessed=1 << 20, transcendentals=0),
        name="precond",
    )(near(acts_low), near(grads_low), near(inv_in), near(inv_out))


def tiles_view(stored, lanes=128):
    store, layers, width = stored.shape
    runs = width // lanes
    return stored.reshape(store, layers, runs, lanes).transpose(0, 2, 1, 3).reshape(store, runs * layers, lanes)


def half_scores(recv_ref, order_ref, tiles_ref, picked, side, emit):
    queries, part, rank = recv_ref.shape
    store = tiles_ref.shape[0]
    width = part * rank
    tile = 256
    ids = lax.broadcasted_iota(jnp.int32, (queries, queries), 0)
    chosen = (ids == order_ref[...]).astype(F32).astype(BF16)
    rows_high, rows_low = pieces(recv_ref[...].reshape(queries, width))
    picked[:queries, :] = dot(chosen, rows_high, TN).astype(BF16)
    picked[queries:, :] = dot(chosen, rows_low, TN).astype(BF16)
    here = pl.ds(pl.multiple_of(side * part, part), part)
    for n in range(store // tile):
        at = slice(n * tile, (n + 1) * tile)
        high, low = pieces(tiles_ref[at, here, :].reshape(tile, width))
        wide = dot(high, picked[...], NT)
        narrow = dot(low, picked[:queries, :], NT)
        emit(n * tile, wide[:, :queries] + (wide[:, queries:] + narrow))


def core_index():
    return lax.rem(lax.axis_index("row"), CORES)


def own_kernel(recv_ref, order_ref, tiles_ref, out_ref, picked):
    def emit(start, scores):
        out_ref[start : start + scores.shape[0], :] = scores

    half_scores(recv_ref, order_ref, tiles_ref, picked, core_index(), emit)


def other_kernel(swapped_ref, order_ref, tiles_ref, own_ref, out_ref, picked):
    slices, sub, half = out_ref.shape
    group = own_ref.shape[1] // slices

    def emit(start, scores):
        tile = scores.shape[0]
        total = (scores + own_ref[start : start + tile, :]).T
        h, c = divmod(start, half)
        out_ref[:, h * group : (h + 1) * group, c : c + tile] = total.reshape(slices, group, tile)

    half_scores(swapped_ref, order_ref, tiles_ref, picked, CORES - 1 - core_index(), emit)


def partial_scores(recv, swapped, order, stored, slices):
    queries, part, rank = recv.shape
    store = stored.shape[0]
    tiles = near(tiles_view(stored))
    order = order.reshape(1, queries)
    scratch = [pltpu.VMEM((2 * queries, part * rank), BF16)]
    own = pl.pallas_call(
        own_kernel,
        in_specs=[WHOLE] * 3,
        out_specs=WHOLE,
        out_shape=pltpu.VMEM((store, queries), F32),
        scratch_shapes=scratch,
        compiler_params=limit(4),
        cost_estimate=pl.CostEstimate(flops=3 * store * queries * part * rank, bytes_accessed=2 * store * part * rank, transcendentals=0),
        name="own_half",
    )(near(recv), order, tiles)
    sub = 8
    return pl.pallas_call(
        other_kernel,
        in_specs=[WHOLE] * 4,
        out_specs=WHOLE,
        out_shape=pltpu.VMEM((slices, sub, store * (queries // slices) // sub), F32),
        scratch_shapes=scratch,
        compiler_params=limit(4),
        name="other_half",
    )(near(swapped), order, tiles, near(own))


def sum_kernel(parts_ref, out_ref):
    total = jnp.sum(parts_ref[...], axis=0)
    group, store = out_ref.shape
    half = parts_ref.shape[2]
    for h in range(store // half):
        out_ref[:, h * half : (h + 1) * half] = total[h * group : (h + 1) * group]


def sum_parts(parts):
    slices, sub, half = parts.shape
    group = 4
    return pl.pallas_call(
        sum_kernel,
        in_specs=[WHOLE],
        out_specs=WHOLE,
        out_shape=jax.ShapeDtypeStruct((group, sub // group * half), F32),
        name="sum_parts",
    )(near(parts))


def per_device(slices, activations, out_grads, proj_in, proj_out, inv_in, inv_out, stored, query_order):
    acts_low, grads_low = projected(activations, out_grads, proj_in, proj_out)
    mine = preconditioned(acts_low, grads_low, inv_in, inv_out, ROWS, slices)
    mine = mine.reshape((-1,) + mine.shape[2:])
    recv = lax.all_to_all(mine, ("row", "feat"), 0, 0, tiled=True)
    swapped = lax.ppermute(recv, "row", [(r, r ^ 1) for r in range(ROWS)])
    parts = partial_scores(recv, swapped, query_order, stored, slices)
    return sum_parts(lax.all_to_all(parts, "feat", 0, 0, tiled=True))


def solution(mesh):
    placed = (
        P(None, ("row", "feat"), None),
        P(None, ("row", "feat"), None),
        P(),
        P(),
        P(),
        P(),
        P("row", None, "feat"),
        P(),
    )
    return jax.shard_map(
        functools.partial(per_device, mesh.shape["feat"]),
        mesh=mesh,
        in_specs=placed,
        out_specs=P("feat", "row"),
        check_vma=False,
    )
```

```python
import functools

import jax
import jax.numpy as jnp
from jax import lax
from jax.experimental import pallas as pl
from jax.experimental.pallas import tpu as pltpu
from jax.sharding import PartitionSpec as P

ROWS, CORES = 4, 2
F32, BF16 = jnp.float32, jnp.bfloat16
NN = (((1,), (0,)), ((), ()))
NT = (((1,), (1,)), ((), ()))
TN = (((0,), (0,)), ((), ()))
MIB = 1024 * 1024
WHOLE = pl.BlockSpec(memory_space=pltpu.VMEM)
ANYWHERE = pl.BlockSpec(memory_space=pl.ANY)


def limit(mib):
    return pltpu.CompilerParams(vmem_limit_bytes=mib * MIB)


def near(x):
    return pltpu.with_memory_space_constraint(x, pltpu.VMEM)


def far(x):
    return pltpu.with_memory_space_constraint(x, pltpu.HBM)


def dot(a, b, dims=NN):
    return lax.dot_general(a, b, dims, preferred_element_type=F32)


def pieces(x):
    high = x.astype(BF16)
    return high, (x - high.astype(F32)).astype(BF16)


def wide_product(x, w, flip=False):
    rows, cols = x.shape[0], w.shape[0 if flip else 1]
    left, right = jnp.concatenate(pieces(x), axis=0), jnp.concatenate(pieces(w), axis=0 if flip else 1)
    both = dot(left, right, NT if flip else NN)
    return (both[rows:, cols:] + both[rows:, :cols]) + both[:rows, cols:] + both[:rows, :cols]


def project_kernel(acts_hbm, pin_hbm, grads_hbm, pout_hbm, acts_low_ref, grads_low_ref, acts, pin, grads, pout, sems):
    layers, tok, width = acts.shape
    rank = pin.shape[1]
    count = sems.shape[1]
    chunk = width // count

    def copies(i):
        at = pl.ds(i * chunk, chunk)
        return [
            pltpu.make_async_copy(acts_hbm.at[:, :, at], acts.at[:, :, at], sems.at[0, i]),
            pltpu.make_async_copy(pin_hbm.at[at, :], pin.at[at, :], sems.at[1, i]),
            pltpu.make_async_copy(grads_hbm.at[:, :, at], grads.at[:, :, at], sems.at[2, i]),
            pltpu.make_async_copy(pout_hbm.at[at, :], pout.at[at, :], sems.at[3, i]),
        ]

    for i in range(count):
        for copy in copies(i):
            copy.start()
    acts_low = grads_low = jnp.zeros((layers * tok, rank), F32)
    for i in range(count):
        for copy in copies(i):
            copy.wait()
        at = slice(i * chunk, (i + 1) * chunk)
        acts_low += wide_product(acts[:, :, at].reshape(layers * tok, chunk), pin[at, :])
        grads_low += wide_product(grads[:, :, at].reshape(layers * tok, chunk), pout[at, :])
    acts_low_ref[...] = acts_low
    grads_low_ref[...] = grads_low


def projected(activations, out_grads, proj_in, proj_out, count=4):
    layers, tok, width = activations.shape
    rank = proj_in.shape[1]
    tokens = pltpu.VMEM((layers, tok, width), F32)
    side = pltpu.VMEM((width, rank), F32)
    return pl.pallas_call(
        project_kernel,
        in_specs=[ANYWHERE] * 4,
        out_specs=[WHOLE] * 2,
        out_shape=[pltpu.VMEM((layers * tok, rank), F32)] * 2,
        scratch_shapes=[tokens, side, tokens, side, pltpu.SemaphoreType.DMA((4, count))],
        compiler_params=limit(12),
        name="projected",
    )(far(activations), far(proj_in), far(out_grads), far(proj_out))


def precond_kernel(acts_low, grads_low, iin, iout, out_ref):
    rows, slices, part, rank = out_ref.shape
    per = CORES * part
    layers = iin.shape[0]
    tok = acts_low.shape[0] // layers
    runs = per // layers
    share = runs // CORES
    for l in range(layers):
        mine = slice(l * tok, (l + 1) * tok)
        right = wide_product(acts_low[mine, :], iin[l])
        left = wide_product(grads_low[mine, :], iout[l], flip=True)
        (left_high, left_low), (right_high, right_low) = pieces(left), pieces(right)
        tall = jnp.concatenate([left_low, left_low, left_high, left_high], axis=0)
        other = jnp.concatenate([right_low, right_high, right_low, right_high], axis=0)
        cond = dot(tall, other, TN).reshape(slices, runs, rank)
        for r in range(rows):
            c = r % CORES
            out_ref[r, :, l * share : (l + 1) * share, :] = cond[:, c * share : (c + 1) * share, :]


def preconditioned(acts_low, grads_low, inv_in, inv_out, rows, slices):
    layers, rank, _ = inv_in.shape
    return pl.pallas_call(
        precond_kernel,
        in_specs=[WHOLE] * 4,
        out_specs=WHOLE,
        out_shape=pltpu.VMEM((rows, slices, layers * (rank // slices) // CORES, rank), F32),
        compiler_params=limit(4),
        cost_estimate=pl.CostEstimate(flops=1 << 33, bytes_accessed=1 << 20, transcendentals=0),
        name="precond",
    )(near(acts_low), near(grads_low), near(inv_in), near(inv_out))


def tiles_view(stored, lanes=128):
    store, layers, width = stored.shape
    runs = width // lanes
    return stored.reshape(store, layers, runs, lanes).transpose(0, 2, 1, 3).reshape(store, runs * layers, lanes)


def half_scores(layers, recv_ref, order_ref, tiles_ref, picked, side, emit):
    queries, part, rank = recv_ref.shape
    store = tiles_ref.shape[0]
    width = part * rank
    tile = 1024
    ids = lax.broadcasted_iota(jnp.int32, (queries, queries), 0)
    chosen = (ids == order_ref[...]).astype(F32).astype(BF16)
    rows = recv_ref[...].reshape(queries, width)
    share = part // layers
    blocks = [(l * share + run) * rank for run in range(share) for l in range(layers)]
    rows_high, rows_low = pieces(jnp.concatenate([rows[:, b : b + rank] for b in blocks], axis=1))
    picked[:queries, :] = dot(chosen, rows_high, TN).astype(BF16)
    picked[queries:, :] = dot(chosen, rows_low, TN).astype(BF16)
    here = pl.ds(pl.multiple_of(side * part, part), part)
    for n in range(store // tile):
        at = slice(n * tile, (n + 1) * tile)
        high, low = pieces(tiles_ref[at, here, :].reshape(tile, width))
        wide = dot(high, picked[...], NT)
        narrow = dot(low, picked[:queries, :], NT)
        emit(n * tile, wide[:, :queries] + (wide[:, queries:] + narrow))


def core_index():
    return lax.rem(lax.axis_index("row"), CORES)


def own_kernel(layers, recv_ref, order_ref, tiles_ref, out_ref, picked):
    def emit(start, scores):
        out_ref[start : start + scores.shape[0], :] = scores

    half_scores(layers, recv_ref, order_ref, tiles_ref, picked, core_index(), emit)


def other_kernel(layers, swapped_ref, order_ref, tiles_ref, own_ref, out_ref, picked):
    slices, sub, half = out_ref.shape
    group = own_ref.shape[1] // slices

    def emit(start, scores):
        tile = scores.shape[0]
        total = (scores + own_ref[start : start + tile, :]).T
        h, c = divmod(start, half)
        out_ref[:, h * group : (h + 1) * group, c : c + tile] = total.reshape(slices, group, tile)

    half_scores(layers, swapped_ref, order_ref, tiles_ref, picked, CORES - 1 - core_index(), emit)


def partial_scores(recv, swapped, order, stored, slices):
    queries, part, rank = recv.shape
    store, layers, _ = stored.shape
    tiles = near(tiles_view(stored))
    order = order.reshape(1, queries)
    scratch = [pltpu.VMEM((2 * queries, part * rank), BF16)]
    own = pl.pallas_call(
        functools.partial(own_kernel, layers),
        in_specs=[WHOLE] * 3,
        out_specs=WHOLE,
        out_shape=pltpu.VMEM((store, queries), F32),
        scratch_shapes=scratch,
        compiler_params=limit(4),
        cost_estimate=pl.CostEstimate(flops=3 * store * queries * part * rank, bytes_accessed=2 * store * part * rank, transcendentals=0),
        name="own_half",
    )(near(recv), order, tiles)
    sub = 8
    return pl.pallas_call(
        functools.partial(other_kernel, layers),
        in_specs=[WHOLE] * 4,
        out_specs=WHOLE,
        out_shape=pltpu.VMEM((slices, sub, store * (queries // slices) // sub), F32),
        scratch_shapes=scratch,
        compiler_params=limit(4),
        name="other_half",
    )(near(swapped), order, tiles, near(own))


def sum_kernel(parts_ref, out_ref):
    total = jnp.sum(parts_ref[...], axis=0)
    group, store = out_ref.shape
    half = parts_ref.shape[2]
    for h in range(store // half):
        out_ref[:, h * half : (h + 1) * half] = total[h * group : (h + 1) * group]


def sum_parts(parts):
    slices, sub, half = parts.shape
    group = 4
    return pl.pallas_call(
        sum_kernel,
        in_specs=[WHOLE],
        out_specs=WHOLE,
        out_shape=jax.ShapeDtypeStruct((group, sub // group * half), F32),
        name="sum_parts",
    )(near(parts))


def per_device(slices, activations, out_grads, proj_in, proj_out, inv_in, inv_out, stored, query_order):
    acts_low, grads_low = projected(activations, out_grads, proj_in, proj_out)
    mine = preconditioned(acts_low, grads_low, inv_in, inv_out, ROWS, slices)
    mine = mine.reshape((-1,) + mine.shape[2:])
    recv = lax.all_to_all(mine, ("row", "feat"), 0, 0, tiled=True)
    swapped = lax.ppermute(recv, "row", [(r, r ^ 1) for r in range(ROWS)])
    parts = partial_scores(recv, swapped, query_order, stored, slices)
    return sum_parts(lax.all_to_all(parts, "feat", 0, 0, tiled=True))


def solution(mesh):
    placed = (
        P(None, ("row", "feat"), None),
        P(None, ("row", "feat"), None),
        P(),
        P(),
        P(),
        P(),
        P("row", None, "feat"),
        P(),
    )
    return jax.shard_map(
        functools.partial(per_device, mesh.shape["feat"]),
        mesh=mesh,
        in_specs=placed,
        out_specs=P("feat", "row"),
        check_vma=False,
    )
```

```python
import functools

import jax
import jax.numpy as jnp
from jax import lax
from jax.experimental import pallas as pl
from jax.experimental.pallas import tpu as pltpu
from jax.sharding import PartitionSpec as P

ROWS, CORES = 4, 2
F32, BF16 = jnp.float32, jnp.bfloat16
NN = (((1,), (0,)), ((), ()))
NT = (((1,), (1,)), ((), ()))
TN = (((0,), (0,)), ((), ()))
MIB = 1024 * 1024
WHOLE = pl.BlockSpec(memory_space=pltpu.VMEM)
ANYWHERE = pl.BlockSpec(memory_space=pl.ANY)


def limit(mib):
    return pltpu.CompilerParams(vmem_limit_bytes=mib * MIB)


def near(x):
    return pltpu.with_memory_space_constraint(x, pltpu.VMEM)


def far(x):
    return pltpu.with_memory_space_constraint(x, pltpu.HBM)


def dot(a, b, dims=NN):
    return lax.dot_general(a, b, dims, preferred_element_type=F32)


def pieces(x):
    high = x.astype(BF16)
    return high, (x - high.astype(F32)).astype(BF16)


def wide_product(x, w, flip=False):
    rows, cols = x.shape[0], w.shape[0 if flip else 1]
    left, right = jnp.concatenate(pieces(x), axis=0), jnp.concatenate(pieces(w), axis=0 if flip else 1)
    both = dot(left, right, NT if flip else NN)
    return (both[rows:, cols:] + both[rows:, :cols]) + both[:rows, cols:] + both[:rows, :cols]


def project_kernel(acts_hbm, pin_hbm, grads_hbm, pout_hbm, acts_low_ref, grads_low_ref, acts, pin, grads, pout, sems):
    layers, tok, width = acts.shape
    rank = pin.shape[1]
    count = sems.shape[1]
    chunk = width // count

    def copies(i):
        at = pl.ds(i * chunk, chunk)
        return [
            pltpu.make_async_copy(acts_hbm.at[:, :, at], acts.at[:, :, at], sems.at[0, i]),
            pltpu.make_async_copy(pin_hbm.at[at, :], pin.at[at, :], sems.at[1, i]),
            pltpu.make_async_copy(grads_hbm.at[:, :, at], grads.at[:, :, at], sems.at[2, i]),
            pltpu.make_async_copy(pout_hbm.at[at, :], pout.at[at, :], sems.at[3, i]),
        ]

    for i in range(count):
        for copy in copies(i):
            copy.start()
    acts_low = grads_low = jnp.zeros((layers * tok, rank), F32)
    for i in range(count):
        for copy in copies(i):
            copy.wait()
        at = slice(i * chunk, (i + 1) * chunk)
        acts_low += wide_product(acts[:, :, at].reshape(layers * tok, chunk), pin[at, :])
        grads_low += wide_product(grads[:, :, at].reshape(layers * tok, chunk), pout[at, :])
    acts_low_ref[...] = acts_low
    grads_low_ref[...] = grads_low


def projected(activations, out_grads, proj_in, proj_out, count=8):
    layers, tok, width = activations.shape
    rank = proj_in.shape[1]
    tokens = pltpu.VMEM((layers, tok, width), F32)
    side = pltpu.VMEM((width, rank), F32)
    return pl.pallas_call(
        project_kernel,
        in_specs=[ANYWHERE] * 4,
        out_specs=[WHOLE] * 2,
        out_shape=[pltpu.VMEM((layers * tok, rank), F32)] * 2,
        scratch_shapes=[tokens, side, tokens, side, pltpu.SemaphoreType.DMA((4, count))],
        compiler_params=limit(12),
        name="projected",
    )(far(activations), far(proj_in), far(out_grads), far(proj_out))


def precond_kernel(acts_low, grads_low, iin, iout, out_ref):
    rows, slices, part, rank = out_ref.shape
    per = CORES * part
    layers = iin.shape[0]
    tok = acts_low.shape[0] // layers
    runs = per // layers
    share = runs // CORES
    mine = [slice(l * tok, (l + 1) * tok) for l in range(layers)]
    rights = [wide_product(acts_low[mine[l], :], iin[l]) for l in range(layers)]
    lefts = [wide_product(grads_low[mine[l], :], iout[l], flip=True) for l in range(layers)]
    for l, (left, right) in enumerate(zip(lefts, rights)):
        (left_high, left_low), (right_high, right_low) = pieces(left), pieces(right)
        tall = jnp.concatenate([left_low, left_low, left_high, left_high], axis=0)
        other = jnp.concatenate([right_low, right_high, right_low, right_high], axis=0)
        cond = dot(tall, other, TN).reshape(slices, runs, rank)
        for r in range(rows):
            c = r % CORES
            out_ref[r, :, l * share : (l + 1) * share, :] = cond[:, c * share : (c + 1) * share, :]


def preconditioned(acts_low, grads_low, inv_in, inv_out, rows, slices):
    layers, rank, _ = inv_in.shape
    return pl.pallas_call(
        precond_kernel,
        in_specs=[WHOLE] * 4,
        out_specs=WHOLE,
        out_shape=pltpu.VMEM((rows, slices, layers * (rank // slices) // CORES, rank), F32),
        compiler_params=limit(4),
        cost_estimate=pl.CostEstimate(flops=1 << 33, bytes_accessed=1 << 20, transcendentals=0),
        name="precond",
    )(near(acts_low), near(grads_low), near(inv_in), near(inv_out))


def tiles_view(stored, lanes=128):
    store, layers, width = stored.shape
    runs = width // lanes
    return stored.reshape(store, layers, runs, lanes).transpose(0, 2, 1, 3).reshape(store, runs * layers, lanes)


def half_scores(layers, recv_ref, order_ref, tiles_ref, picked, side, emit):
    queries, part, rank = recv_ref.shape
    store = tiles_ref.shape[0]
    width = part * rank
    tile = 1024
    ids = lax.broadcasted_iota(jnp.int32, (queries, queries), 0)
    chosen = (ids == order_ref[...]).astype(F32).astype(BF16)
    rows = recv_ref[...].reshape(queries, width)
    share = part // layers
    blocks = [(l * share + run) * rank for run in range(share) for l in range(layers)]
    rows_high, rows_low = pieces(jnp.concatenate([rows[:, b : b + rank] for b in blocks], axis=1))
    picked[:queries, :] = dot(chosen, rows_high, TN).astype(BF16)
    picked[queries:, :] = dot(chosen, rows_low, TN).astype(BF16)
    here = pl.ds(pl.multiple_of(side * part, part), part)
    for n in range(store // tile):
        at = slice(n * tile, (n + 1) * tile)
        high, low = pieces(tiles_ref[at, here, :].reshape(tile, width))
        wide = dot(high, picked[...], NT)
        narrow = dot(low, picked[:queries, :], NT)
        emit(n * tile, wide[:, :queries] + (wide[:, queries:] + narrow))


def core_index():
    return lax.rem(lax.axis_index("row"), CORES)


def own_kernel(layers, recv_ref, order_ref, tiles_ref, out_ref, picked):
    def emit(start, scores):
        out_ref[start : start + scores.shape[0], :] = scores

    half_scores(layers, recv_ref, order_ref, tiles_ref, picked, core_index(), emit)


def other_kernel(layers, swapped_ref, order_ref, tiles_ref, own_ref, out_ref, picked):
    slices, sub, half = out_ref.shape
    group = own_ref.shape[1] // slices

    def emit(start, scores):
        tile = scores.shape[0]
        total = (scores + own_ref[start : start + tile, :]).T
        h, c = divmod(start, half)
        out_ref[:, h * group : (h + 1) * group, c : c + tile] = total.reshape(slices, group, tile)

    half_scores(layers, swapped_ref, order_ref, tiles_ref, picked, CORES - 1 - core_index(), emit)


def partial_scores(recv, swapped, order, stored, slices):
    queries, part, rank = recv.shape
    store, layers, _ = stored.shape
    tiles = near(tiles_view(stored))
    order = order.reshape(1, queries)
    scratch = [pltpu.VMEM((2 * queries, part * rank), BF16)]
    own = pl.pallas_call(
        functools.partial(own_kernel, layers),
        in_specs=[WHOLE] * 3,
        out_specs=WHOLE,
        out_shape=pltpu.VMEM((store, queries), F32),
        scratch_shapes=scratch,
        compiler_params=limit(4),
        cost_estimate=pl.CostEstimate(flops=3 * store * queries * part * rank, bytes_accessed=2 * store * part * rank, transcendentals=0),
        name="own_half",
    )(near(recv), order, tiles)
    sub = 8
    return pl.pallas_call(
        functools.partial(other_kernel, layers),
        in_specs=[WHOLE] * 4,
        out_specs=WHOLE,
        out_shape=pltpu.VMEM((slices, sub, store * (queries // slices) // sub), F32),
        scratch_shapes=scratch,
        compiler_params=limit(4),
        name="other_half",
    )(near(swapped), order, tiles, near(own))


def sum_kernel(parts_ref, out_ref):
    total = jnp.sum(parts_ref[...], axis=0)
    group, store = out_ref.shape
    half = parts_ref.shape[2]
    for h in range(store // half):
        out_ref[:, h * half : (h + 1) * half] = total[h * group : (h + 1) * group]


def sum_parts(parts):
    slices, sub, half = parts.shape
    group = 4
    return pl.pallas_call(
        sum_kernel,
        in_specs=[WHOLE],
        out_specs=WHOLE,
        out_shape=jax.ShapeDtypeStruct((group, sub // group * half), F32),
        name="sum_parts",
    )(near(parts))


def per_device(slices, activations, out_grads, proj_in, proj_out, inv_in, inv_out, stored, query_order):
    acts_low, grads_low = projected(activations, out_grads, proj_in, proj_out)
    mine = preconditioned(acts_low, grads_low, inv_in, inv_out, ROWS, slices)
    mine = mine.reshape((-1,) + mine.shape[2:])
    recv = lax.all_to_all(mine, ("row", "feat"), 0, 0, tiled=True)
    swapped = lax.ppermute(recv, "row", [(r, r ^ 1) for r in range(ROWS)])
    parts = partial_scores(recv, swapped, query_order, stored, slices)
    return sum_parts(lax.all_to_all(parts, "feat", 0, 0, tiled=True))


def solution(mesh):
    placed = (
        P(None, ("row", "feat"), None),
        P(None, ("row", "feat"), None),
        P(),
        P(),
        P(),
        P(),
        P("row", None, "feat"),
        P(),
    )
    return jax.shard_map(
        functools.partial(per_device, mesh.shape["feat"]),
        mesh=mesh,
        in_specs=placed,
        out_specs=P("feat", "row"),
        check_vma=False,
    )
```
